32 devices in a mesh: seq: 8 (over z, x), head: 4 (over y, core).
Axes of the slice: x: 2, y: 2, z: 4, core: 2. Of those that a mesh axis runs over, the one named last changes fastest.
Arguments:
- queries: bfloat16 [8192, 2048], P('seq', 'head'), may hold values from -6 to 6
- keys: bfloat16 [8192, 2048], P('seq', 'head'), may hold values from -6 to 6
- values: bfloat16 [8192, 2048], P('seq', 'head'), may hold values from -6 to 6
- feature_proj: bfloat16 [2, 16, 128, 16], P(None, 'head'), may hold values from -0.5 to 0.5
- lin_gain: float32 [2048], P('head'), may hold values from 0.5 to 1.5
- win_gain: float32 [2048], P('head'), may hold values from 0.5 to 1.5
- out_proj: bfloat16 [2048, 2048], P('head'), may hold values from -0.1875 to 0.1875
- block_list: int32 [8, 4, 3], replicated, may hold values from -4 to 7, as said below
Outputs:
- mixed: bfloat16 [8192, 2048], P('seq', 'head')
The draws below stay inside these ranges and needn't reach their ends.
Inputs may be any that keep to these rules, and one draw needn't show every extreme that they name: `block_list`: entry [s, r - 1] has first column s - r; its third column (a number of blocks) is 0 where s - r < 0, else 1 to 4, and equals 4 in every entry of some shard in every draw; the run of blocks starting at the second column stays inside shard s - r, and for r = 1 it ends at least 128 tokens before that shard's end.
All inputs are finite; a program needn't handle non-finite values.
Results may differ from the reference program's by a relative error of at most 0.013.
Values may be sent and summed in bfloat16 or wider, within the bound.
No kernel may reach another device: no remote copies, remote signals or barrier semaphores. Data moves between devices by JAX's collectives and lax.ppermute only.
A program may use at most 128 MiB of HBM per device.

```python
import jax
import jax.numpy as jnp
from jax import lax

D = 2048
HEADS = 16
HD = 128
FD = 16
FEAT = 273
TOK_DEV = 1024
BLK = 128
WIN = 128
REACH = 4
CAP = 4
TOKENS = 8192
N_SEQ = 8
N_HEAD = 4


def drawn_pair(key):
    streams = jax.random.split(jax.random.fold_in(key, 11), 2)
    query_draw = jnp.clip(jax.random.normal(streams[0], (TOKENS, D), jnp.float32), -3.0, 3.0)
    key_draw = jnp.clip(jax.random.normal(streams[1], (TOKENS, D), jnp.float32), -3.0, 3.0)
    return (query_draw, key_draw)


def draw_queries(key, part):
    return drawn_pair(key)[0].astype(jnp.bfloat16)


def draw_keys(key, part):
    return drawn_pair(key)[1].astype(jnp.bfloat16)


def draw_values(key, part):
    streams = jax.random.split(jax.random.fold_in(key, 23), 2)
    head_of = jnp.arange(D) // HD
    column_scale = 0.5 * 4.0 ** ((head_of + jax.random.uniform(streams[0], (D,), jnp.float32)) / HEADS)
    entries = jnp.clip(jax.random.normal(streams[1], (TOKENS, D), jnp.float32), -3.0, 3.0)
    return (entries * column_scale[None, :]).astype(jnp.bfloat16)


def draw_block_list(key, part):
    streams = jax.random.split(jax.random.fold_in(key, 37), 4)
    per_shard = TOK_DEV // BLK
    shard_ids = jnp.arange(N_SEQ)[:, None]
    reach_ids = jnp.arange(1, REACH + 1)[None, :]
    source_ids = shard_ids - reach_ids
    run_length = jax.random.randint(streams[1], (N_SEQ, REACH), 1, CAP + 1)
    full_shard = jax.random.randint(streams[2], (), REACH, N_SEQ)
    run_length = jnp.where(shard_ids == full_shard, CAP, run_length)
    run_length = jnp.where(source_ids < 0, 0, run_length)
    upper_end = jnp.where(reach_ids == 1, per_shard - WIN // BLK, per_shard)
    first_block = jax.random.randint(streams[3], (N_SEQ, REACH), 0, upper_end - jnp.maximum(run_length, 1) + 1)
    source_full = jnp.broadcast_to(source_ids, (N_SEQ, REACH))
    return jnp.stack([source_full, first_block, run_length], axis=-1).astype(jnp.int32)


def strengthened(values, key, source, target, parts, factor):
    def block_of(axis_at):
        return (jnp.arange(values.shape[axis_at]) // (values.shape[axis_at] // parts)).reshape((-1,) + (1,) * (values.ndim - 1 - axis_at))

    near = jax.random.permutation(key, parts)[block_of(target)]
    far = (block_of(target) + parts // 2) % parts
    return jnp.where((block_of(source) == near) | (block_of(source) == far), factor * values, values)


def shard_levels(key, dims, cuts, smallest, top_value):
    factor_of = 1.0
    for axis_at, parts in cuts:
        steps = jax.random.uniform(jax.random.fold_in(jax.random.fold_in(key, 6), axis_at), (parts,), jnp.float32, smallest / len(cuts), top_value / len(cuts))
        factor_of = factor_of * jnp.repeat(jnp.exp(steps), dims[axis_at] // parts).reshape((-1,) + (1,) * (len(dims) - 1 - axis_at))
    return factor_of


def bell_draw(own_key, extent, deviation, reach, cuts=(), kind=jnp.bfloat16):
    loudness = shard_levels(own_key, extent, cuts, -0.22, 0.18) if cuts else 1.0
    result = jax.random.normal(own_key, extent, jnp.float32) * deviation * loudness
    return jnp.minimum(jnp.maximum(result, -reach), reach).astype(kind)


def noise_with(rng, dims, scale, bound, shards, heavy, kind=jnp.bfloat16):
    values = scale * jax.random.normal(rng, dims, jnp.float32)
    if shards:
        values = values * shard_levels(rng, dims, shards, -0.22, 0.18)
    return jnp.clip(strengthened(values, jax.random.fold_in(rng, 3), *heavy), -bound, bound).astype(kind)


def setup_inputs(seed: int = 0) -> dict:
    arg_keys = jax.random.split(jax.random.key(seed), 9)
    queries = draw_queries(jax.random.fold_in(arg_keys[8], 71), 0)
    keys = draw_keys(jax.random.fold_in(arg_keys[8], 71), 0)
    values = draw_values(jax.random.fold_in(arg_keys[8], 71), 0)
    feature_proj = bell_draw(arg_keys[3], (2, HEADS, HD, FD), HD ** -0.5, 0.5, ((1, 4),))
    lin_gain = jnp.clip(1.0 + 0.1 * jax.random.normal(arg_keys[4], (D,), jnp.float32), 0.5, 1.5)
    win_gain = jnp.clip(1.0 + 0.1 * jax.random.normal(arg_keys[5], (D,), jnp.float32), 0.5, 1.5)
    out_proj = noise_with(arg_keys[6], (D, D), D ** -0.5, 0.1875, ((0, 4),), (0, 1, 4, 2.0))
    block_list = draw_block_list(jax.random.fold_in(arg_keys[8], 71), 0)
    return dict(queries=queries, keys=keys, values=values, feature_proj=feature_proj, lin_gain=lin_gain, win_gain=win_gain, out_proj=out_proj, block_list=block_list)


def feature_map(inputs):
    leading = inputs.shape[:-1]
    breadth = inputs.shape[-1]
    squares = (inputs[..., :, None] * inputs[..., None, :]).reshape(leading + (breadth * breadth,)) * 0.5 ** 0.5
    return jnp.concatenate([jnp.ones(leading + (1,), inputs.dtype), inputs, squares], axis=-1)

def head_norm(arrays):
    return arrays * lax.rsqrt(lax.optimization_barrier(jnp.mean(arrays * arrays, axis=-1, keepdims=True)) + 1e-06)

def reference(queries, keys, values, feature_proj, lin_gain, win_gain, out_proj, block_list):
    high = lax.Precision.HIGHEST
    per_shard = TOK_DEV // BLK
    remote_rows = REACH * CAP * BLK
    proj_float = feature_proj.astype(jnp.float32)
    shaped_q = queries.reshape(N_SEQ, TOK_DEV, HEADS, HD)
    shaped_k = keys.reshape(N_SEQ, TOK_DEV, HEADS, HD)
    shaped_v = values.reshape(N_SEQ, TOK_DEV, HEADS, HD)
    lin_scale = lin_gain.reshape(HEADS, 1, HD)
    win_scale = win_gain.reshape(HEADS, 1, HD)

    def one_shard(states, inputs):
        shard_q, shard_k, shard_v, entries, shard = inputs
        q_float = shard_q.astype(jnp.float32)
        k_float = shard_k.astype(jnp.float32)
        v_heads = jnp.transpose(shard_v.astype(jnp.float32), (1, 0, 2))
        q_feat = jnp.einsum('thd,hdf->htf', q_float, proj_float[0], precision=high) * FD ** (-0.25)
        k_feat = jnp.einsum('thd,hdf->htf', k_float, proj_float[1], precision=high) * FD ** (-0.25)
        phi_query = lax.optimization_barrier(feature_map(q_feat).astype(jnp.bfloat16)).astype(jnp.float32)
        phi_key = lax.optimization_barrier(feature_map(k_feat).astype(jnp.bfloat16)).astype(jnp.float32)
        kernel = jnp.einsum('htf,hsf->hts', phi_query, phi_key, precision=high)
        causal = jnp.arange(TOK_DEV)[None, :] <= jnp.arange(TOK_DEV)[:, None]
        weights = lax.optimization_barrier(jnp.where(causal[None], kernel, 0.0).astype(jnp.bfloat16)).astype(jnp.float32)
        linear = jnp.einsum('hts,hsd->htd', weights, v_heads, precision=high) + jnp.einsum('htf,hfd->htd', phi_query, states, precision=high)
        new_states = states + jnp.einsum('htf,htd->hfd', phi_key, v_heads, precision=high)
        start = (shard * TOK_DEV).astype(jnp.int32)
        rim_start = jnp.maximum(start - WIN, 0).astype(jnp.int32)
        piece_k = [lax.dynamic_slice_in_dim(keys, rim_start, WIN, 0), lax.dynamic_slice_in_dim(keys, start, TOK_DEV, 0)]
        piece_v = [lax.dynamic_slice_in_dim(values, rim_start, WIN, 0), lax.dynamic_slice_in_dim(values, start, TOK_DEV, 0)]
        usable_all = []
        for offset in range(REACH):
            source_shard = jnp.maximum(entries[offset, 0], 0)
            first_block = entries[offset, 1]
            run_length = entries[offset, 2]
            begin = jnp.minimum(first_block, per_shard - CAP)
            row_start = ((source_shard * per_shard + begin) * BLK).astype(jnp.int32)
            piece_k.append(lax.dynamic_slice_in_dim(keys, row_start, CAP * BLK, 0))
            piece_v.append(lax.dynamic_slice_in_dim(values, row_start, CAP * BLK, 0))
            block_ids = begin + jnp.arange(CAP)
            usable = (block_ids >= first_block) & (block_ids < first_block + run_length)
            usable_all.append(jnp.repeat(usable, BLK))
        key_set = jnp.concatenate(piece_k, 0).astype(jnp.float32).reshape(-1, HEADS, HD)
        value_set = jnp.concatenate(piece_v, 0).astype(jnp.float32).reshape(-1, HEADS, HD)
        key_pos = start - WIN + jnp.arange(WIN + TOK_DEV)
        query_pos = start + jnp.arange(TOK_DEV)
        in_window = (key_pos[None, :] > query_pos[:, None] - WIN) & (key_pos[None, :] <= query_pos[:, None]) & (key_pos[None, :] >= 0)
        remote_ok = jnp.concatenate(usable_all)
        allowed = jnp.concatenate([in_window, jnp.broadcast_to(remote_ok[None, :], (TOK_DEV, remote_rows))], axis=1)
        scores = jnp.einsum('thd,shd->hts', q_float, key_set, precision=high) * HD ** (-0.5)
        scores = jnp.where(allowed[None], scores, -jnp.inf)
        row_max = lax.optimization_barrier(jnp.max(scores, axis=-1, keepdims=True))
        raised = jnp.exp(scores - row_max)
        probs = lax.optimization_barrier((raised / lax.optimization_barrier(jnp.sum(raised, axis=-1, keepdims=True))).astype(jnp.bfloat16)).astype(jnp.float32)
        window = jnp.einsum('hts,shd->htd', probs, value_set, precision=high)
        head_out = win_scale * head_norm(window) + lin_scale * head_norm(linear)
        flat = jnp.transpose(head_out, (1, 0, 2)).reshape(TOK_DEV, HEADS * HD).astype(jnp.bfloat16)
        return (new_states, flat)
    carry = jnp.zeros((HEADS, FEAT, HD), jnp.float32)
    shard_ids = jnp.arange(N_SEQ).astype(jnp.int32)
    carry_end, blocks = lax.scan(one_shard, carry, (shaped_q, shaped_k, shaped_v, block_list, shard_ids))
    head_rows = blocks.reshape(TOKENS, D)
    group_cols = D // N_HEAD
    summed = jnp.zeros((TOKENS, D), jnp.float32)
    for member in range(N_HEAD):
        partial_sum = jnp.dot(head_rows[:, member * group_cols:(member + 1) * group_cols], out_proj[member * group_cols:(member + 1) * group_cols], preferred_element_type=jnp.float32)
        summed = summed + lax.optimization_barrier(partial_sum.astype(jnp.bfloat16)).astype(jnp.float32)
    return summed.astype(jnp.bfloat16)
```

```python
import functools

import jax
import jax.numpy as jnp
from jax import lax
from jax.experimental import pallas as pl
from jax.experimental.pallas import tpu as pltpu
from jax.sharding import PartitionSpec as P

FD = 16
BLK = 128
WIN = 128
REACH = 4
CAP = 4
HD = 128
LISTED = CAP * BLK
QUAD = FD * (FD // 2 + 1)
FEATS = QUAD + 2 * FD
QT = 256
EXTRA = 16
LOG2E = 1.4426950408889634
SCALE2 = HD ** (-0.5) * LOG2E
NEG = -1e30
BIG = 1e30
F32 = jnp.float32
BF16 = jnp.bfloat16
VMEM = 56 * 1024 * 1024
ANY = pl.BlockSpec(memory_space=pl.ANY)


def nt(a, b):
    return lax.dot_general(a, b, (((1,), (1,)), ((), ())), preferred_element_type=F32)


def tn(a, b):
    return lax.dot_general(a, b, (((0,), (0,)), ((), ())), preferred_element_type=F32)


def params():
    return pltpu.CompilerParams(vmem_limit_bytes=VMEM)


def cost(flops, nbytes):
    return pl.CostEstimate(flops=int(flops), bytes_accessed=int(nbytes), transcendentals=0)


def entry(listing, shards, per_shard, dest, reach):
    inside = dest < shards
    at = jnp.minimum(dest, shards - 1)
    first = listing[at, reach - 1, 1]
    count = jnp.where(inside, listing[at, reach - 1, 2], 0)
    begin = jnp.clip(first, 0, per_shard - CAP)
    return begin, first, count


def valid_flags(begin, first, count):
    return [(begin + b >= first) & (begin + b < first + count) for b in range(CAP)]


def gather_kernel(chunks, width, shards, listing, where, q, k, v, *rest):
    outs, sems = rest[:-1], rest[-1]
    rows = k.shape[0]
    per_shard = rows // BLK
    shard = where[0]
    copies = []

    def copy(src, dst):
        copies.append(pltpu.make_async_copy(src, dst, sems.at[len(copies)]))

    for c in range(chunks):
        near, far, pair, mine = outs[4 * c : 4 * c + 4]
        cols = pl.ds(c * width, width)
        for i, kv in enumerate((k, v)):
            to = pl.ds(i * width, width)
            copy(kv.at[pl.ds(rows - WIN, WIN), cols], near.at[pl.ds(0, WIN), to])
            for reach, dst, base in ((3, near, WIN), (4, far, 0), (1, pair, 0)):
                begin, _, _ = entry(listing, shards, per_shard, shard + reach, reach)
                start = pl.multiple_of(begin * BLK, BLK)
                copy(kv.at[pl.ds(start, LISTED), cols], dst.at[pl.ds(base, LISTED), to])
        copy(q.at[:, cols], mine)
    for one in copies:
        one.start()
    for one in copies:
        one.wait()


def gather(listing, where, q, k, v, chunks, width, shards):
    rows = q.shape[0]
    shapes = []
    for _ in range(chunks):
        shapes += [
            jax.ShapeDtypeStruct((WIN + LISTED, 2 * width), BF16),
            jax.ShapeDtypeStruct((LISTED, 2 * width), BF16),
            jax.ShapeDtypeStruct((LISTED, 2 * width), BF16),
            jax.ShapeDtypeStruct((rows, width), BF16),
        ]
    return pl.pallas_call(
        functools.partial(gather_kernel, chunks, width, shards),
        grid_spec=pltpu.PrefetchScalarGridSpec(
            num_scalar_prefetch=2,
            grid=(1,),
            in_specs=[ANY] * 3,
            out_specs=[ANY] * len(shapes),
            scratch_shapes=[pltpu.SemaphoreType.DMA((9 * chunks,))],
        ),
        out_shape=shapes,
        compiler_params=pltpu.CompilerParams(vmem_limit_bytes=4 * 1024 * 1024),
        name="gather_rows",
    )(listing, where, q, k, v)


def features(wide, shifted, rows):
    row = lax.broadcasted_iota(jnp.int32, (FEATS, 1), 0)
    root = FD ** (-0.25)
    edge = (row < FD) | ((row >= QUAD - FD) & (row < QUAD))
    scale_left = jnp.where(edge, root * 0.5**0.5, root)
    add_left = jnp.where(row == QUAD + FD, 1.0, 0.0)
    add_right = jnp.where((row >= QUAD) & (row <= QUAD + FD), 1.0, 0.0)
    left = nt(wide, rows) * scale_left + add_left
    right = nt(shifted, rows) * root + add_right
    return (left * right).astype(BF16)


def linear_kernel(q, k, v, wide, shifted, proj, out, state, qs, ks):
    rows = q.shape[0]
    root = FD ** (-0.25)
    lane = lax.broadcasted_iota(jnp.int32, (1, 3 * FD), 1) // FD
    for ref, src, which, low in ((qs, q, 0, 1), (ks, k, 1, 2)):
        feat = jnp.dot(src[...], proj[which, 0], preferred_element_type=F32) * root
        high = feat.astype(BF16)
        rest = (feat - high.astype(F32)).astype(BF16)
        ref[...] = jnp.where(lane == low, rest.astype(F32), high.astype(F32)).astype(BF16)
    phi = features(wide[1, 0], shifted[1, 0], k[...])
    state[0] = jnp.dot(phi, v[...], preferred_element_type=F32)
    key_at = lax.broadcasted_iota(jnp.int32, (QT, QT), 0)
    query_at = lax.broadcasted_iota(jnp.int32, (QT, QT), 1)
    for i in range(rows // QT):
        here = pl.ds(i * QT, QT)
        acc = jnp.zeros((HD, QT), F32)
        for j in range(i + 1):
            there = pl.ds(j * QT, QT)
            dot = nt(ks[there, :], qs[here, :])
            weights = (0.5 * dot + 1.0) * dot + 1.0
            if i == j:
                weights = jnp.where(key_at <= query_at, weights, 0.0)
            acc += tn(v[there, :], weights.astype(BF16))
        out[0, :, here] = acc


def linear(q, k, v, wide, shifted, proj):
    rows, heads = q.shape[0], wide.shape[1]
    col = pl.BlockSpec((rows, HD), lambda h: (0, h))
    return pl.pallas_call(
        linear_kernel,
        grid=(heads,),
        in_specs=[
            col,
            col,
            col,
            pl.BlockSpec((2, 1, FEATS, HD), lambda h: (0, h, 0, 0)),
            pl.BlockSpec((2, 1, FEATS, HD), lambda h: (0, h, 0, 0)),
            pl.BlockSpec((2, 1, HD, 3 * FD), lambda h: (0, h, 0, 0)),
        ],
        out_specs=[
            pl.BlockSpec((1, HD, rows), lambda h: (h, 0, 0)),
            pl.BlockSpec((1, FEATS, HD), lambda h: (h, 0, 0)),
        ],
        out_shape=[
            jax.ShapeDtypeStruct((heads, HD, rows), F32),
            jax.ShapeDtypeStruct((heads, FEATS, HD), F32),
        ],
        scratch_shapes=[pltpu.VMEM((rows, 3 * FD), BF16), pltpu.VMEM((rows, 3 * FD), BF16)],
        compiler_params=params(),
        cost_estimate=cost(heads * 3e9, heads * rows * HD * 10),
        name="linear_local",
    )(q, k, v, wide, shifted, proj)


def attend(sources, queries):
    scores, best = [], None
    for keys, _, flags in sources:
        s = nt(keys, queries)
        scores.append(s)
        for b, flag in enumerate(flags):
            top = jnp.max(s[b * BLK : (b + 1) * BLK], axis=0, keepdims=True)
            top = jnp.where(flag, top, NEG)
            best = top if best is None else jnp.maximum(best, top)
    best = best * SCALE2
    total, acc = None, None
    for s, (_, values, flags) in zip(scores, sources):
        parts = []
        for b, flag in enumerate(flags):
            shift = jnp.where(flag, best, BIG)
            p = jnp.exp2(s[b * BLK : (b + 1) * BLK] * SCALE2 - shift)
            part = jnp.sum(p, axis=0, keepdims=True)
            total = part if total is None else total + part
            parts.append(p.astype(BF16))
        product = tn(values, jnp.concatenate(parts, axis=0))
        acc = product if acc is None else acc + product
    return best, total, acc


def listed_kernel(shards, per_shard, listing, where, q, k, v, nk, nv, fk, fv, pk, pv, out):
    shard = where[0]
    dest = shard + 2
    even = shard % 2 == 0
    pair = valid_flags(*entry(listing, shards, per_shard, dest, 1))
    own_entry = entry(listing, shards, per_shard, dest, 2)
    near = valid_flags(*entry(listing, shards, per_shard, dest, 3))
    far = valid_flags(*entry(listing, shards, per_shard, dest, 4))
    begin = pl.multiple_of(own_entry[0] * BLK, BLK)
    own = valid_flags(*own_entry)
    rows = q.shape[0]

    def run(with_pair):
        def tile(i, carry):
            here = pl.ds(pl.multiple_of(i * QT, QT), QT)
            sources = [
                (k[pl.ds(begin, LISTED), :], v[pl.ds(begin, LISTED), :], own),
                (nk[pl.ds(WIN, LISTED), :], nv[pl.ds(WIN, LISTED), :], near),
                (fk[...], fv[...], far),
            ]
            if with_pair:
                sources.append((pk[...], pv[...], pair))
            best, total, acc = attend(sources, q[here, :])
            safe = jnp.maximum(total, 1e-30)
            out[0, 0:HD, here] = (acc / safe).astype(BF16)
            level = jnp.where(total > 0.0, best + jnp.log2(safe), NEG)
            high = level.astype(BF16).astype(F32)
            mid = (level - high).astype(BF16).astype(F32)
            low = level - high - mid
            row = lax.broadcasted_iota(jnp.int32, (EXTRA, QT), 0)
            packed = jnp.where(row == 0, high, jnp.where(row == 1, mid, jnp.where(row == 2, low, 0.0)))
            out[0, HD : HD + EXTRA, here] = packed.astype(BF16)
            return carry

        lax.fori_loop(0, rows // QT, tile, 0)

    pl.when(even)(lambda: run(True))
    pl.when(jnp.logical_not(even))(lambda: run(False))


def listed(listing, where, q_got, k, v, near, far, pair, first_head, heads, shards):
    rows = k.shape[0]
    per_shard = rows // BLK

    def cols(n, base):
        return pl.BlockSpec((n, HD), lambda h, *_: (0, base + h))

    return pl.pallas_call(
        functools.partial(listed_kernel, shards, per_shard),
        grid_spec=pltpu.PrefetchScalarGridSpec(
            num_scalar_prefetch=2,
            grid=(heads,),
            in_specs=[
                cols(rows, 0),
                cols(rows, first_head),
                cols(rows, first_head),
                cols(WIN + LISTED, 0),
                cols(WIN + LISTED, heads),
                cols(LISTED, 0),
                cols(LISTED, heads),
                cols(LISTED, 0),
                cols(LISTED, heads),
            ],
            out_specs=pl.BlockSpec((1, HD + EXTRA, rows), lambda h, *_: (h, 0, 0)),
        ),
        out_shape=jax.ShapeDtypeStruct((heads, HD + EXTRA, rows), BF16),
        compiler_params=params(),
        cost_estimate=cost(heads * 4e9, heads * rows * HD * 10),
        name="listed_attention",
    )(listing, where, q_got, k, v, near, near, far, far, pair, pair)


def window_kernel(shards, per_shard, listing, where, q, k, v, nk, nv, pk, pv, out, level):
    shard = where[0]
    rows = q.shape[0]
    flags = valid_flags(*entry(listing, shards, per_shard, shard, 1))
    key_at = lax.broadcasted_iota(jnp.int32, (QT + WIN, QT), 0)
    query_at = lax.broadcasted_iota(jnp.int32, (QT + WIN, QT), 1)
    band = (key_at > query_at) & (key_at <= query_at + WIN)

    def window(i, queries):
        if i == 0:
            keys = jnp.concatenate([nk[0:WIN, :], k[0:QT, :]], axis=0)
            values = jnp.concatenate([nv[0:WIN, :], v[0:QT, :]], axis=0)
            mask = band & ((shard > 0) | (key_at >= WIN))
        else:
            at = pl.ds(i * QT - WIN, QT + WIN)
            keys, values, mask = k[at, :], v[at, :], band
        s = jnp.where(mask, nt(keys, queries) * SCALE2, NEG)
        best = jnp.max(s, axis=0, keepdims=True)
        p = jnp.exp2(s - best)
        return best, jnp.sum(p, axis=0, keepdims=True), tn(values, p.astype(BF16))

    def store(here, best, total, acc):
        out[0, :, here] = acc / total
        level[0, :, here] = jnp.broadcast_to(best + jnp.log2(total), (8, QT))

    def run(with_pair):
        for i in range(rows // QT):
            here = pl.ds(i * QT, QT)
            queries = q[here, :]
            best, total, acc = window(i, queries)
            if with_pair:
                best2, total2, acc2 = attend([(pk[...], pv[...], flags)], queries)
                top = jnp.maximum(best, best2)
                one, two = jnp.exp2(best - top), jnp.exp2(best2 - top)
                best, total, acc = top, total * one + total2 * two, acc * one + acc2 * two
            store(here, best, total, acc)

    odd = shard % 2 == 1
    pl.when(odd)(lambda: run(True))
    pl.when(jnp.logical_not(odd))(lambda: run(False))


def window(listing, where, q, k, v, near, pair, first_head, heads, shards):
    rows = k.shape[0]
    per_shard = rows // BLK

    def cols(n, base):
        return pl.BlockSpec((n, HD), lambda h, *_: (0, base + h))

    return pl.pallas_call(
        functools.partial(window_kernel, shards, per_shard),
        grid_spec=pltpu.PrefetchScalarGridSpec(
            num_scalar_prefetch=2,
            grid=(heads,),
            in_specs=[
                cols(rows, first_head),
                cols(rows, first_head),
                cols(rows, first_head),
                cols(WIN, 0),
                cols(WIN, heads),
                cols(LISTED, 0),
                cols(LISTED, heads),
            ],
            out_specs=[
                pl.BlockSpec((1, HD, rows), lambda h, *_: (h, 0, 0)),
                pl.BlockSpec((1, 8, rows), lambda h, *_: (h, 0, 0)),
            ],
        ),
        out_shape=[
            jax.ShapeDtypeStruct((heads, HD, rows), F32),
            jax.ShapeDtypeStruct((heads, 8, rows), F32),
        ],
        compiler_params=params(),
        cost_estimate=cost(heads * 2e9, heads * rows * HD * 10),
        name="window_attention",
    )(listing, where, q, k, v, near, near, pair, pair)


def combine_kernel(where, q, win, win_level, got, lin, before, wide, shifted, win_gain, lin_gain, out):
    shard = where[0]
    phi = features(wide[0, 0], shifted[0, 0], q[...])
    linear = lin[0] + tn(before[0].astype(BF16), phi)
    packed = got[0, HD : HD + EXTRA, :].astype(F32)
    level = packed[0:1] + packed[1:2] + packed[2:3]
    level = jnp.where(shard >= 2, level, NEG)
    mine = win_level[0, 0:1, :]
    top = jnp.maximum(level, mine)
    one, two = jnp.exp2(mine - top), jnp.exp2(level - top)
    inverse = 1.0 / (one + two)
    window = win[0] * (one * inverse) + got[0, 0:HD, :].astype(F32) * (two * inverse)

    def norm(x):
        return x * lax.rsqrt(jnp.mean(x * x, axis=0, keepdims=True) + 1e-06)

    result = win_gain[0] * norm(window) + lin_gain[0] * norm(linear)
    out[...] = result.T.astype(BF16)


def combine(where, q, win, win_level, got, lin, before, wide, shifted, win_gain, lin_gain, first_head, heads):
    rows = q.shape[0]

    def local(*dims):
        return pl.BlockSpec((1, *dims), lambda h, *_: (h, 0, 0))

    def whole(*dims):
        return pl.BlockSpec((1, *dims), lambda h, *_: (first_head + h, 0, 0))

    weights = pl.BlockSpec((1, 1, FEATS, HD), lambda h, *_: (0, first_head + h, 0, 0))
    return pl.pallas_call(
        combine_kernel,
        grid_spec=pltpu.PrefetchScalarGridSpec(
            num_scalar_prefetch=1,
            grid=(heads,),
            in_specs=[
                pl.BlockSpec((rows, HD), lambda h, *_: (0, first_head + h)),
                local(HD, rows),
                local(8, rows),
                local(HD + EXTRA, rows),
                whole(HD, rows),
                whole(FEATS, HD),
                weights,
                weights,
                whole(HD, 1),
                whole(HD, 1),
            ],
            out_specs=pl.BlockSpec((rows, HD), lambda h, *_: (0, h)),
        ),
        out_shape=jax.ShapeDtypeStruct((rows, heads * HD), BF16),
        compiler_params=params(),
        cost_estimate=cost(heads * 5e8, heads * rows * HD * 10),
        name="combine_heads",
    )(where, q, win, win_level, got, lin, before, wide, shifted, win_gain, lin_gain)


def project_kernel(count, last, *refs):
    parts, weights = refs[:count], refs[count : 2 * count]
    out = refs[-1]
    acc = None if len(refs) == 2 * count + 1 else refs[-2][...]
    for a, w in zip(parts, weights):
        product = jnp.dot(a[...], w[...], preferred_element_type=F32)
        acc = product if acc is None else acc + product
    out[...] = acc.astype(out.dtype)


def project(parts, weights, chunk, before, last):
    rows, width = parts[0].shape
    columns = weights[0].shape[1]
    tile = min(256, rows)
    count = len(parts)
    specs = [pl.BlockSpec((tile, width), lambda i: (i, 0))] * count
    specs += [pl.BlockSpec((width, columns), lambda i: (chunk, 0))] * count
    args = list(parts) + list(weights)
    block = pl.BlockSpec((tile, columns), lambda i: (i, 0))
    if before is not None:
        specs.append(block)
        args.append(before)
    return pl.pallas_call(
        functools.partial(project_kernel, count, last),
        grid=(rows // tile,),
        in_specs=specs,
        out_specs=block,
        out_shape=jax.ShapeDtypeStruct((rows, columns), BF16 if last else F32),
        compiler_params=params(),
        cost_estimate=cost(2 * count * rows * width * columns, 8 * rows * columns),
        name="project",
    )(*args)


def moved(x, axis, by):
    n = lax.axis_size(axis)
    return lax.ppermute(x, axis, [(i, i + by) for i in range(n) if 0 <= i + by < n])


def swapped(x, axis, mask):
    return lax.ppermute(x, axis, [(i, i ^ mask) for i in range(lax.axis_size(axis))])


def local(queries, keys, values, feature_proj, lin_gain, win_gain, out_proj, block_list):
    rows, columns = queries.shape
    heads = feature_proj.shape[1]
    shards = lax.axis_size("seq")
    groups = lax.axis_size("head")
    shard = lax.axis_index("seq")
    group = lax.axis_index("head")
    where = jnp.reshape(shard, (1,)).astype(jnp.int32)
    chunks = 2
    per = heads // chunks
    width = per * HD

    sent = gather(block_list, where, queries, keys, values, chunks, width, shards)
    got = []
    for c in range(chunks):
        near, far, pair, mine = sent[4 * c : 4 * c + 4]
        got.append(
            (
                moved(near, "seq", 1),
                moved(far, "seq", 2),
                swapped(pair, "seq", 1),
                moved(mine, "seq", -2),
            )
        )

    turned = jnp.transpose(feature_proj, (0, 1, 3, 2))
    none = jnp.zeros_like(turned)
    wide = jnp.concatenate([turned] * (FD // 2 + 2) + [none], axis=2)
    shifted = jnp.concatenate(
        [jnp.roll(turned, -d, axis=2) for d in range(FD // 2 + 1)] + [none, none], axis=2
    )
    tripled = jnp.concatenate([feature_proj] * 3, axis=-1)
    lin, state = linear(queries, keys, values, wide, shifted, tripled)

    other = swapped(state.astype(BF16), "seq", 1).astype(F32)
    both = state + other
    before = jnp.zeros_like(both)
    step = 2
    while step < shards:
        before = before + moved((both + before).astype(BF16), "seq", step).astype(F32)
        step *= 2
    before = before + jnp.where(shard % 2 == 1, other, 0.0)

    masks = [0]
    bit = groups // 2
    while bit:
        masks = masks + [m ^ bit for m in masks]
        bit //= 2
    out_columns = out_proj.shape[1] // groups
    weights = []
    for m in masks:
        piece = lax.dynamic_slice_in_dim(out_proj, (group ^ m) * out_columns, out_columns, 1)
        weights.append(swapped(piece, "head", m) if m else piece)

    win_column = win_gain.reshape(heads, HD, 1)
    lin_column = lin_gain.reshape(heads, HD, 1)
    total = None
    for c in range(chunks):
        near, far, pair, mine = got[c]
        away = listed(block_list, where, mine, keys, values, near, far, pair, c * per, per, shards)
        back = moved(away, "seq", 2)
        win, level = window(block_list, where, queries, keys, values, near, pair, c * per, per, shards)
        part = combine(
            where, queries, win, level, back, lin, before, wide, shifted, win_column, lin_column, c * per, per
        )
        parts = [part]
        bit = groups // 2
        while bit:
            parts = parts + [swapped(p, "head", bit) for p in parts]
            bit //= 2
        total = project(parts, weights, c, total, c == chunks - 1)
    return total


def solution(mesh):
    in_specs = (
        P("seq", "head"),
        P("seq", "head"),
        P("seq", "head"),
        P(None, "head", None, None),
        P("head"),
        P("head"),
        P("head", None),
        P(),
    )
    return jax.shard_map(local, mesh=mesh, in_specs=in_specs, out_specs=P("seq", "head"), check_vma=False)
```
